256 devices in a mesh: img: 4 (over y_hi, core), row: 8 (over z), col: 8 (over y_lo, x).
Axes of the slice: x: 4, y: 4 (y_hi: 2, y_lo: 2; y = y_hi * 2 + y_lo), z: 8, core: 2. Of those that a mesh axis runs over, the one named last changes fastest.
Arguments:
- fresh: bfloat16 [256, 128, 640], P(('img', 'row'), 'col'), parts along dimension 0, may hold values from -16 to 16
- stale_conv_in: bfloat16 [256, 128, 640], P(('img', 'row'), 'col'), parts along dimension 0, may hold values from -6 to 6
- stale_normed: bfloat16 [256, 128, 640], P(('img', 'row'), 'col'), parts along dimension 0, may hold values from -6 to 6
- norm_gain: float32 [640], replicated, may hold values from 0.5 to 1.5
- conv_weight: bfloat16 [3, 3, 640, 640], replicated, may hold values from -0.078125 to 0.078125
- attn_gain: float32 [640], replicated, may hold values from 0.5 to 1.5
- w_query: bfloat16 [640, 640], replicated, may hold values from -3 to 3
- w_key: bfloat16 [640, 640], replicated, may hold values from -3 to 3
- w_value: bfloat16 [640, 640], replicated, may hold values from -0.25 to 0.25
- w_out: bfloat16 [640, 640], replicated, may hold values from -0.625 to 0.625
Outputs:
- result: bfloat16 [256, 128, 640], P(('img', 'row'), 'col'), parts along dimension 0
The draws below stay inside these ranges and needn't reach their ends.
There are 4 independent parts, one for each index of `img`. The reference program is written for one: setup_inputs(seed, part) draws one part's arguments, and reference() takes and returns one part's arrays. A program takes and returns all parts, laid end to end along the dimension named above; an argument that names none is the same for every part. Nothing has to cross between parts.
All inputs are finite; a program needn't handle non-finite values.
Results may differ from the reference program's by a relative error of at most 0.017.
The reference program's roundings to bfloat16 on the way (of `conv_in`, `normed`, `query`, `weight` and `attended`) count: a program that leaves them out, or rounds other values in their place, can miss the bound.
Values may be sent and summed in bfloat16 or wider, within the bound.
A program may use at most 128 MiB of HBM per device.

```python
import math
import jax
import jax.numpy as jnp
from jax import lax

C = 640
GROUPS = 32
HEAD = 64
PH = 8
PW = 16
HEADS = 10
H = 64
W = 128
KEYS = 8192
N_ROW = 8
N_COL = 8


def head_factor(key, low, high):
    first, second = jax.random.split(key)
    level = jax.random.uniform(first, (HEADS,), jnp.float32, math.log(low), math.log(high))
    chosen = jax.random.randint(second, (), 0, HEADS)
    level = jnp.where(jnp.arange(HEADS) == chosen, math.log(high), level)
    return jnp.repeat(jnp.exp(level), HEAD).astype(jnp.float32)


def draw_w_query(key, part):
    factor = head_factor(key, 1.5, 3.0)
    key = jax.random.fold_in(key, 11)
    base = jnp.clip(jax.random.normal(key, (C, C), jnp.float32), -3.0, 3.0) * C ** (-0.5)
    return (base * factor[None, :]).astype(jnp.bfloat16)


def draw_w_key(key, part):
    factor = head_factor(key, 1.5, 3.0)
    key = jax.random.fold_in(key, 12)
    base = jnp.clip(jax.random.normal(key, (C, C), jnp.float32), -3.0, 3.0) * C ** (-0.5)
    return (base * factor[None, :]).astype(jnp.bfloat16)


def draw_fresh(key, part):
    key = jax.random.fold_in(key, 13)
    row_scale = 3.0 ** (jnp.arange(H, dtype=jnp.float32) / (H - 1))
    base = jnp.clip(jax.random.normal(key, (H, W, C), jnp.float32), -4.0, 4.0)
    base = base * row_scale[:, None, None]
    return base.astype(jnp.bfloat16)


def steps_of(rng, dims, cuts, least, largest):
    def one(axis_at, parts):
        heights = jax.random.uniform(jax.random.fold_in(jax.random.fold_in(rng, 6), axis_at), (parts,), jnp.float32, least / len(cuts), largest / len(cuts))
        return jnp.repeat(jnp.exp(heights), dims[axis_at] // parts).reshape((-1,) + (1,) * (len(dims) - axis_at - 1))

    level = one(*cuts[0])
    for cut in cuts[1:]:
        level = level * one(*cut)
    return level


def centred(key, shape, width, most, pieces=(), kind=jnp.bfloat16):
    values = width * jax.random.normal(key, shape, jnp.float32)
    if pieces:
        values = values * steps_of(key, shape, pieces, -0.22, 0.18)
    return jnp.clip(values, -most, most).astype(kind)


def setup_inputs(seed: int = 0, part: int = 0) -> dict:
    splits = jax.random.split(jax.random.key(seed), 11)
    part_keys = jax.random.split(jax.random.fold_in(splits[10], part), 11)
    fresh = draw_fresh(jax.random.fold_in(jax.random.fold_in(splits[10], part), 71), part)
    stale_conv_in = centred(part_keys[1], (H, W, C), 1.0, 6.0, ((0, 8), (1, 8)))
    stale_normed = centred(part_keys[2], (H, W, C), 1.0, 6.0, ((0, 8), (1, 8)))
    norm_gain = jnp.clip(1.0 + 0.1 * jax.random.normal(splits[3], (C,), jnp.float32), 0.5, 1.5)
    conv_weight = centred(splits[4], (3, 3, C, C), (9 * C) ** -0.5, 0.078125)
    attn_gain = jnp.clip(1.0 + 0.1 * jax.random.normal(splits[5], (C,), jnp.float32), 0.5, 1.5)
    w_query = draw_w_query(jax.random.fold_in(splits[10], 71), part)
    w_key = draw_w_key(jax.random.fold_in(splits[10], 71), part)
    w_value = centred(splits[8], (C, C), C ** -0.5, 0.25)
    w_out = centred(splits[9], (C, C), (C // 8) ** -0.5, 0.625)
    return {"fresh": fresh, "stale_conv_in": stale_conv_in, "stale_normed": stale_normed, "norm_gain": norm_gain, "conv_weight": conv_weight, "attn_gain": attn_gain, "w_query": w_query, "w_key": w_key, "w_value": w_value, "w_out": w_out}


def to_patches(arr):
    return arr.reshape(N_ROW, PH, N_COL, PW, C).transpose(0, 2, 1, 3, 4).reshape(N_ROW * N_COL, PH * PW, C)

def from_patches(arr):
    return arr.reshape(N_ROW, N_COL, PH, PW, C).transpose(0, 2, 1, 3, 4).reshape(H, W, C)

def reference(fresh, stale_conv_in, stale_normed, norm_gain, conv_weight, attn_gain, w_query, w_key, w_value, w_out):
    x = fresh.astype(jnp.float32)
    grouped = x.reshape(H, W, GROUPS, C // GROUPS)
    count = H * W * (C // GROUPS)
    mean_g = lax.optimization_barrier(jnp.sum(grouped, axis=(0, 1, 3))) / count
    msq_g = lax.optimization_barrier(jnp.sum(grouped * grouped, axis=(0, 1, 3))) / count
    var_g = msq_g - mean_g * mean_g
    normed_g = (grouped - mean_g[None, None, :, None]) * lax.rsqrt(var_g + 1e-05)[None, None, :, None]
    conv_in = jax.nn.silu(normed_g.reshape(H, W, C) * norm_gain).astype(jnp.bfloat16)
    pad_fresh = jnp.pad(conv_in, ((1, 1), (1, 1), (0, 0)))
    pad_stale = jnp.pad(stale_conv_in, ((1, 1), (1, 1), (0, 0)))
    rows_i = jnp.arange(H, dtype=jnp.int32)
    cols_j = jnp.arange(W, dtype=jnp.int32)
    total = jnp.zeros((H * W, C), jnp.float32)
    for tap_a in range(3):
        for tap_b in range(3):
            same_r = (rows_i + tap_a - 1 + PH) // PH == (rows_i + PH) // PH
            same_c = (cols_j + tap_b - 1 + PW) // PW == (cols_j + PW) // PW
            same = same_r[:, None] & same_c[None, :]
            shifted = jnp.where(same[:, :, None], pad_fresh[tap_a:tap_a + H, tap_b:tap_b + W], pad_stale[tap_a:tap_a + H, tap_b:tap_b + W])
            total = total + jnp.dot(shifted.reshape(H * W, C), conv_weight[tap_a, tap_b], preferred_element_type=jnp.float32)
    hidden = x + total.reshape(H, W, C)
    mean = lax.optimization_barrier(jnp.mean(hidden, axis=-1, keepdims=True))
    var = lax.optimization_barrier(jnp.mean((hidden - mean) ** 2, axis=-1, keepdims=True))
    normed = ((hidden - mean) * lax.rsqrt(var + 1e-05) * attn_gain).astype(jnp.bfloat16)
    tok_normed = to_patches(normed).reshape(KEYS, C)
    tok_stale = to_patches(stale_normed).reshape(KEYS, C)
    query = jnp.dot(tok_normed, w_query, preferred_element_type=jnp.float32).astype(jnp.bfloat16)
    own_key = jnp.dot(tok_normed, w_key, preferred_element_type=jnp.float32).astype(jnp.bfloat16)
    own_value = jnp.dot(tok_normed, w_value, preferred_element_type=jnp.float32).astype(jnp.bfloat16)
    stale_key = jnp.dot(tok_stale, w_key, preferred_element_type=jnp.float32).astype(jnp.bfloat16)
    stale_value = jnp.dot(tok_stale, w_value, preferred_element_type=jnp.float32).astype(jnp.bfloat16)
    key_patch = jnp.arange(KEYS, dtype=jnp.int32) // (PH * PW)
    query_blocks = query.reshape(N_ROW * N_COL, PH * PW, HEADS, HEAD)

    def one_patch(index):
        chosen = (key_patch == index)[:, None]
        keys = jnp.where(chosen, own_key, stale_key).reshape(KEYS, HEADS, HEAD)
        values = jnp.where(chosen, own_value, stale_value).reshape(KEYS, HEADS, HEAD)
        block = query_blocks[index]
        score = jnp.einsum('qhd,khd->hqk', block.astype(jnp.float32), keys.astype(jnp.float32)) * 0.125
        top = lax.optimization_barrier(jnp.max(score, axis=-1, keepdims=True))
        expo = jnp.exp(score - top)
        denom = lax.optimization_barrier(jnp.sum(expo, axis=-1))
        weight = expo.astype(jnp.bfloat16)
        summed = jnp.einsum('hqk,khd->hqd', weight.astype(jnp.float32), values.astype(jnp.float32))
        attended = (summed / denom[:, :, None]).transpose(1, 0, 2).reshape(PH * PW, C)
        return attended.astype(jnp.bfloat16)
    attended = lax.map(one_patch, jnp.arange(N_ROW * N_COL, dtype=jnp.int32))
    projected = jnp.dot(attended.reshape(KEYS, C), w_out, preferred_element_type=jnp.float32)
    result = to_patches(hidden).reshape(KEYS, C) + projected
    return from_patches(result.reshape(N_ROW * N_COL, PH * PW, C)).astype(jnp.bfloat16)
```

```python
import functools
import jax
import jax.numpy as jnp
from jax import lax
from jax.experimental import pallas as pl
from jax.experimental.pallas import tpu as pltpu
from jax.sharding import PartitionSpec as P

GROUPS = 32
HEAD = 64
C = 640
TOK = 128
PW = 16
NZ = 8
NX = 4
NCOL = 8
PAIRS = 5
KROWS = 17 * TOK
SPAN = 16 * TOK
LOG2E = 1.4426950408889634
MESH = pl.DeviceIdType.MESH
F32 = jnp.float32
BF16 = jnp.bfloat16
HIGH = lax.Precision.HIGHEST
NT = (((1,), (1,)), ((), ()))
TN = (((0,), (0,)), ((), ()))


def iota(shape, dim):
    return lax.broadcasted_iota(jnp.int32, shape, dim)


def kernel(
    fresh_h, sci_h, sn_h, ngain, again, wc_h, wq_h, wk_h, wv_h, wo_h,
    out_ref,
    fresh, sci, wc, wq, wkv, wo,
    st_send, st_recv,
    colbuf, ext, xw,
    sb, kall, vx, hid,
    q_mine, q_recv, part, ret_a, lse, ret_l,
    load_sem, st_ssem, st_rsem, halo_ssem, halo_rsem,
    zo_ssem, zo_rsem, zp_ssem, zp_rsem, y_ssem, y_rsem,
    q_ssem, q_rsem, a_ssem, a_rsem, l_ssem, l_rsem,
):
    r = lax.axis_index("row")
    c = lax.axis_index("col")
    x = lax.rem(c, NX)
    ybase = c - x
    rown = [lax.rem(r + j, NZ) for j in range(NZ)]
    coln = [lax.rem(c + j, NCOL) for j in range(NCOL)]
    xn = [ybase + lax.rem(x + j, NX) for j in range(NX)]
    ypart = lax.rem(c + NX, NCOL)

    def remote(src, dst, ss, rs, dev):
        return pltpu.make_async_remote_copy(
            src_ref=src, dst_ref=dst, send_sem=ss, recv_sem=rs,
            device_id=dev, device_id_type=MESH)

    loads = [
        pltpu.make_async_copy(fresh_h, fresh, load_sem.at[0]),
        pltpu.make_async_copy(sn_h, sb.at[0, pl.ds(0, TOK)], load_sem.at[1]),
        pltpu.make_async_copy(sci_h, sci, load_sem.at[2]),
        pltpu.make_async_copy(wk_h, wkv.at[:, pl.ds(0, C)], load_sem.at[3]),
        pltpu.make_async_copy(wv_h, wkv.at[:, pl.ds(C, C)], load_sem.at[4]),
        pltpu.make_async_copy(wc_h, wc, load_sem.at[5]),
        pltpu.make_async_copy(wq_h, wq, load_sem.at[6]),
        pltpu.make_async_copy(wo_h, wo, load_sem.at[7]),
    ]
    for cp in loads:
        cp.start()

    barrier = pltpu.get_barrier_semaphore()
    partners = [{"row": rown[j]} for j in range(1, NZ)]
    partners += [{"col": coln[j]} for j in range(1, NCOL)]
    partners += [{"row": rown[i], "col": coln[j]} for i in (1, NZ - 1) for j in (1, NCOL - 1)]
    for dev in partners:
        pl.semaphore_signal(barrier, inc=1, device_id=dev, device_id_type=MESH)

    loads[0].wait()
    xf = fresh[...].astype(F32)
    s1 = jnp.sum(xf, axis=0, keepdims=True)
    s2 = jnp.sum(xf * xf, axis=0, keepdims=True)
    row8 = iota((8, C), 0)
    st = jnp.where(row8 == 0, s1, jnp.where(row8 == 1, s2, 0.0))
    per = C // GROUPS
    gc = iota((C, 128), 0)
    gl = iota((C, 128), 1) * per
    gmat = jnp.where((gc >= gl) & (gc < gl + per), 1.0, 0.0).astype(F32)
    st_send[0] = jnp.dot(st, gmat, precision=HIGH, preferred_element_type=F32)
    loads[2].wait()
    e0 = iota((16, TOK), 0)
    e1 = iota((16, TOK), 1)
    want = jnp.where(e0 < 8, e0 * PW, (e0 - 8) * PW + PW - 1)
    sel = jnp.where(e1 == want, 1.0, 0.0).astype(BF16)
    colbuf[...] = jnp.dot(sel, sci[...], preferred_element_type=F32).astype(BF16)
    loads[1].wait()

    pl.semaphore_wait(barrier, len(partners))

    def stat_copies(stage):
        devs = [{"row": rown[j]} if stage == 0 else {"col": coln[j]} for j in range(1, 8)]
        return [remote(st_send.at[stage], st_recv.at[stage, j], st_ssem.at[stage, j], st_rsem.at[stage, j], dev)
                for j, dev in enumerate(devs)]

    stat1 = stat_copies(0)
    for cp in stat1:
        cp.start()

    up, down = {"row": rown[1]}, {"row": rown[NZ - 1]}

    def own_copy(step, plus):
        src = step - 1 if plus else (0 if step == 1 else 3 + step)
        dst = step if plus else 4 + step
        i = step - 1 + (0 if plus else 4)
        return remote(sb.at[src, pl.ds(0, TOK)], sb.at[dst, pl.ds(0, TOK)],
                      zo_ssem.at[i], zo_rsem.at[i], up if plus else down)

    def half_copy(step, plus):
        src = step - 1 if plus else (0 if step == 1 else 3 + step)
        dst = step if plus or step == 4 else 4 + step
        i = step - 1 + (0 if plus else 4)
        return remote(sb.at[src, pl.ds(TOK, 64)], sb.at[dst, pl.ds(TOK, 64)],
                      zp_ssem.at[i], zp_rsem.at[i], up if plus else down)

    def y_copy(slot):
        return remote(sb.at[slot, pl.ds(64, 64)], sb.at[slot, pl.ds(TOK + 64, 64)],
                      y_ssem.at[slot], y_rsem.at[slot], {"col": ypart})

    y_first = remote(sb.at[0, pl.ds(0, 64)], sb.at[0, pl.ds(TOK, 64)],
                     y_ssem.at[8], y_rsem.at[8], {"col": ypart})
    own_p = {s: own_copy(s, True) for s in range(1, 5)}
    own_m = {s: own_copy(s, False) for s in range(1, 4)}
    half_p = {s: half_copy(s, True) for s in range(1, 4)}
    half_m = {s: half_copy(s, False) for s in range(1, 5)}
    ys = {s: y_copy(s) for s in range(8)}
    y_first.start()
    own_p[1].start()
    own_m[1].start()

    lft, rgt = coln[NCOL - 1], coln[1]
    upr, dnr = rown[NZ - 1], rown[1]
    top, bot = sci.at[pl.ds(0, 16)], sci.at[pl.ds(TOK - 16, 16)]
    plan = [
        (top, 144, {"row": upr}), (top, 240, {"row": upr, "col": lft}), (top, 224, {"row": upr, "col": rgt}),
        (bot, 0, {"row": dnr}), (bot, 208, {"row": dnr, "col": lft}), (bot, 192, {"row": dnr, "col": rgt}),
        (colbuf, 176, {"col": lft}), (colbuf, 160, {"col": rgt}),
    ]
    halos = [remote(src, ext.at[pl.ds(at, 16)], halo_ssem.at[i], halo_rsem.at[i], dev)
             for i, (src, at, dev) in enumerate(plan)]
    for cp in halos:
        cp.start()
    ys[0].start()

    for p in range(PAIRS):
        vx[:, 256 * p + 128:256 * p + 256] = jnp.ones((KROWS, 128), BF16)

    def project(block, rows):
        kv = jnp.dot(block, wkv[...], preferred_element_type=F32).astype(BF16)
        for i, row in enumerate(rows):
            piece = kv[i * TOK:(i + 1) * TOK]
            kall[row:row + TOK, :] = piece[:, :C]
            for p in range(PAIRS):
                vx[row:row + TOK, 256 * p:256 * p + 128] = piece[:, C + 128 * p:C + 128 * p + 128]

    def own_rows(slot):
        return sb[slot, 0:TOK]

    def far_rows(slot):
        return sb[slot, TOK:2 * TOK]

    loads[3].wait()
    loads[4].wait()
    project(own_rows(0), [16 * TOK])

    tot = st_send[0]
    for j, cp in enumerate(stat1):
        cp.wait_recv()
        tot = tot + st_recv[0, j]
    st_send[1] = tot
    stat2 = stat_copies(1)
    for cp in stat2:
        cp.start()
    y_first.wait_recv()
    half_p[1].start()
    half_m[1].start()

    pe = iota((160, 256), 0)
    ps = iota((160, 256), 1)
    pi = lax.shift_right_logical(pe, 4)
    pj = pe & 15
    inner = (pi > 0) & (pi < 9)
    vert = ((pi > 0) | (r > 0)) & ((pi < 9) | (r < NZ - 1))
    left_src = jnp.where(pj > 0, pe - 1, jnp.where(inner, 167 + pi, jnp.where(pi == 0, 207, 239)))
    right_src = jnp.where(pj < 15, pe + 1, jnp.where(inner, 175 + pi, jnp.where(pi == 0, 208, 240)))
    left_ok = vert & ((pj > 0) | (c > 0))
    right_ok = vert & ((pj < 15) | (c < NCOL - 1))
    sel_left = jnp.where(left_ok & (ps == left_src), 1.0, 0.0).astype(BF16)
    sel_right = jnp.where(right_ok & (ps == right_src), 1.0, 0.0).astype(BF16)

    own_p[1].wait_recv()
    own_m[1].wait_recv()
    own_p[2].start()
    own_m[2].start()
    ys[1].start()
    ys[5].start()
    project(jnp.concatenate([own_rows(1), own_rows(5)], axis=0), [TOK, 5 * TOK])

    tot = st_send[1]
    for j, cp in enumerate(stat2):
        cp.wait_recv()
        tot = tot + st_recv[1, j]
    count = TOK * NZ * NCOL * per
    mom = tot * (1.0 / count)
    mean_g = mom[0:1]
    var_g = mom[1:2] - mean_g * mean_g
    rstd_g = lax.rsqrt(var_g + 1e-05)
    row8 = iota((8, 128), 0)
    both = jnp.where(row8 == 0, mean_g, jnp.where(row8 == 1, rstd_g, 0.0))
    hl = iota((128, C), 0) * per
    hc = iota((128, C), 1)
    gback = jnp.where((hc >= hl) & (hc < hl + per), 1.0, 0.0).astype(F32)
    wide = jnp.dot(both, gback, precision=HIGH, preferred_element_type=F32)
    xf = fresh[...].astype(F32)
    v = (xf - wide[0:1]) * wide[1:2] * ngain[...]
    ext[16:16 + TOK, :] = (v * (1.0 / (1.0 + jnp.exp(-v)))).astype(BF16)
    for cp in halos:
        cp.wait_recv()
    zero = jnp.zeros((16, C), BF16)
    ext[0:16, :] = jnp.where(r > 0, ext[0:16, :], zero)
    ext[144:160, :] = jnp.where(r < NZ - 1, ext[144:160, :], zero)
    whole = ext[...]
    e_left = jnp.dot(sel_left, whole, preferred_element_type=F32).astype(BF16)
    e_right = jnp.dot(sel_right, whole, preferred_element_type=F32).astype(BF16)
    for a in range(3):
        xw[:, (3 * a) * C:(3 * a + 1) * C] = e_left[16 * a:16 * a + TOK]
        xw[:, (3 * a + 1) * C:(3 * a + 2) * C] = ext[16 * a:16 * a + TOK, :]
        xw[:, (3 * a + 2) * C:(3 * a + 3) * C] = e_right[16 * a:16 * a + TOK]
    loads[5].wait()
    hidden = xf + jnp.dot(xw[...], wc[...], preferred_element_type=F32)
    hid[...] = hidden
    mean = jnp.mean(hidden, axis=-1, keepdims=True)
    cen = hidden - mean
    var = jnp.mean(cen * cen, axis=-1, keepdims=True)
    normed = (cen * lax.rsqrt(var + 1e-05) * again[...]).astype(BF16)
    loads[6].wait()
    q_mine[...] = (jnp.dot(normed, wq[...], preferred_element_type=F32) * (LOG2E / 8)).astype(BF16)
    q_cp = {j: remote(q_mine, q_recv.at[NX - j - 1], q_ssem.at[j - 1], q_rsem.at[NX - j - 1], {"col": xn[j]})
            for j in (1, 3, 2)}
    for cp in q_cp.values():
        cp.start()
    project(normed, [0])

    half_p[1].wait_recv()
    half_m[1].wait_recv()
    half_p[2].start()
    half_m[2].start()
    own_p[2].wait_recv()
    own_m[2].wait_recv()
    own_p[3].start()
    own_m[3].start()
    ys[2].start()
    ys[6].start()
    project(jnp.concatenate([own_rows(2), own_rows(6)], axis=0), [2 * TOK, 6 * TOK])
    half_p[2].wait_recv()
    half_m[2].wait_recv()
    half_p[3].start()
    half_m[3].start()
    own_p[3].wait_recv()
    own_m[3].wait_recv()
    own_p[4].start()
    ys[3].start()
    ys[7].start()
    project(jnp.concatenate([own_rows(3), own_rows(7)], axis=0), [3 * TOK, 7 * TOK])
    half_m[3].wait_recv()
    half_m[4].start()
    half_p[3].wait_recv()
    for s in (0, 1, 5):
        ys[s].wait_recv()
    project(jnp.concatenate([far_rows(0), far_rows(1), far_rows(5)], axis=0), [8 * TOK, 9 * TOK, 13 * TOK])
    own_p[4].wait_recv()
    ys[4].start()
    for s in (2, 6, 3, 7):
        ys[s].wait_recv()
    project(jnp.concatenate([far_rows(s) for s in (2, 6, 3, 7)], axis=0), [(8 + s) * TOK for s in (2, 6, 3, 7)])
    half_m[4].wait_recv()
    ys[4].wait_recv()
    project(jnp.concatenate([own_rows(4), far_rows(4)], axis=0), [4 * TOK, 12 * TOK])

    lane = iota((TOK, 128), 1)

    def attend(read_q, base, write, lse_ref):
        table = jnp.zeros((TOK, 128), F32)
        for p in range(PAIRS):
            qp = read_q(p)
            zq = jnp.zeros_like(qp)
            qm = jnp.concatenate([jnp.where(lane < HEAD, qp, zq), jnp.where(lane < HEAD, zq, qp)], axis=0)
            s = lax.dot_general(qm, kall[base:base + SPAN, 128 * p:128 * p + 128], NT, preferred_element_type=F32)
            m = jnp.max(s, axis=1, keepdims=True)
            w = jnp.exp2(s - m).astype(BF16)
            o = jnp.dot(w, vx[base:base + SPAN, 256 * p:256 * p + 256], preferred_element_type=F32)
            den = o[:, 128:]
            norm = o[:, :128] / den
            write(p, jnp.where(lane < HEAD, norm[:TOK], norm[TOK:]).astype(BF16))
            ls = m + jnp.log2(den)
            table = jnp.where(lane == 2 * p, ls[:TOK], jnp.where(lane == 2 * p + 1, ls[TOK:], table))
        lse_ref[...] = table.T[:16]

    def writer(ref):
        def write(p, val):
            ref[:, 128 * p:128 * p + 128] = val
        return write

    def reader(ref):
        return lambda p: ref[:, 128 * p:128 * p + 128]

    attend(reader(q_mine), 0, writer(part.at[0]), lse.at[0])
    backs = []
    for j in (1, 3, 2):
        q_cp[NX - j].wait_recv()
        attend(reader(q_recv.at[j - 1]), TOK, writer(part.at[j]), lse.at[j])
        dst = NX - j - 1
        a_cp = remote(part.at[j], ret_a.at[dst], a_ssem.at[j - 1], a_rsem.at[dst], {"col": xn[j]})
        l_cp = remote(lse.at[j], ret_l.at[dst], l_ssem.at[j - 1], l_rsem.at[dst], {"col": xn[j]})
        a_cp.start()
        l_cp.start()
        backs += [a_cp, l_cp]
    for cp in backs:
        cp.wait_recv()

    ls = [lse[0]] + [ret_l[j] for j in range(3)]
    top_l = jnp.maximum(jnp.maximum(ls[0], ls[1]), jnp.maximum(ls[2], ls[3]))
    ws = [jnp.exp2(l - top_l) for l in ls]
    inv = 1.0 / (ws[0] + ws[1] + ws[2] + ws[3])
    eh = iota((32, C), 0) & 15
    ec = iota((32, C), 1)
    spread = jnp.where((ec >= eh * HEAD) & (ec < eh * HEAD + HEAD), 1.0, 0.0).astype(BF16)
    att = jnp.zeros((TOK, C), F32)
    for i in range(4):
        share = ws[i] * inv
        hi = share.astype(BF16)
        lo = (share - hi.astype(F32)).astype(BF16)
        split = jnp.concatenate([hi, lo], axis=0)
        full = lax.dot_general(split, spread, TN, preferred_element_type=F32)
        val = part[0] if i == 0 else ret_a[i - 1]
        att = att + full * val.astype(F32)
    loads[7].wait()
    out = hid[...] + jnp.dot(att.astype(BF16), wo[...], preferred_element_type=F32)
    out_ref[...] = out.astype(BF16)

    sends = stat1 + stat2 + halos + [y_first] + list(own_p.values()) + list(own_m.values())
    sends += list(half_p.values()) + list(half_m.values()) + list(ys.values()) + list(q_cp.values()) + backs
    for cp in sends:
        cp.wait_send()


def on_device(fresh, stale_conv_in, stale_normed, norm_gain, conv_weight, attn_gain, w_query, w_key, w_value, w_out):
    shape = fresh.shape
    flat = lambda a: a.reshape(TOK, C)
    hbm = pl.BlockSpec(memory_space=pl.ANY)
    vmem = pl.BlockSpec(memory_space=pltpu.VMEM)
    dma = pltpu.SemaphoreType.DMA
    V = pltpu.VMEM
    out = pl.pallas_call(
        kernel,
        out_shape=jax.ShapeDtypeStruct((TOK, C), BF16),
        in_specs=[hbm] * 3 + [vmem] * 2 + [hbm] * 5,
        out_specs=vmem,
        scratch_shapes=[
            V((TOK, C), BF16), V((TOK, C), BF16), V((9 * C, C), BF16), V((C, C), BF16), V((C, 2 * C), BF16), V((C, C), BF16),
            V((2, 8, 128), F32), V((2, 7, 8, 128), F32),
            V((16, C), BF16), V((256, C), BF16), V((TOK, 9 * C), BF16),
            V((NZ, 2 * TOK, C), BF16), V((KROWS, C), BF16), V((KROWS, 256 * PAIRS), BF16), V((TOK, C), F32),
            V((TOK, C), BF16), V((3, TOK, C), BF16), V((4, TOK, C), BF16), V((3, TOK, C), BF16),
            V((4, 16, 128), F32), V((3, 16, 128), F32),
            dma((8,)), dma((2, 7)), dma((2, 7)), dma((8,)), dma((8,)),
            dma((8,)), dma((8,)), dma((8,)), dma((8,)), dma((9,)), dma((9,)),
            dma((3,)), dma((3,)), dma((3,)), dma((3,)), dma((3,)), dma((3,)),
        ],
        compiler_params=pltpu.CompilerParams(
            collective_id=0, has_side_effects=True, vmem_limit_bytes=60 * 2**20),
    )(
        flat(fresh), flat(stale_conv_in), flat(stale_normed),
        norm_gain.reshape(1, C), attn_gain.reshape(1, C),
        conv_weight.reshape(9 * C, C), w_query, w_key, w_value, w_out,
    )
    return out.reshape(shape)


def solution(mesh):
    cells = P(("img", "row"), "col", None)
    return jax.shard_map(
        on_device,
        mesh=mesh,
        in_specs=(cells, cells, cells) + (P(),) * 7,
        out_specs=cells,
        check_vma=False,
    )
```

```python
import functools
import jax
import jax.numpy as jnp
from jax import lax
from jax.experimental import pallas as pl
from jax.experimental.pallas import tpu as pltpu
from jax.sharding import PartitionSpec as P

GROUPS = 32
HEAD = 64
C = 640
TOK = 128
PW = 16
NZ = 8
NX = 4
NCOL = 8
PAIRS = 5
KROWS = 17 * TOK
ORDER = [None, (0, 1), (0, 5), (0, 2), (0, 6), (1, 0), (1, 1), (1, 5), (0, 0),
         (0, 3), (0, 7), (1, 2), (1, 6), (0, 4), (1, 3), (1, 7), (1, 4)]
LOG2E = 1.4426950408889634
MESH = pl.DeviceIdType.MESH
F32 = jnp.float32
BF16 = jnp.bfloat16
HIGH = lax.Precision.HIGHEST
NT = (((1,), (1,)), ((), ()))
TN = (((0,), (0,)), ((), ()))


def iota(shape, dim):
    return lax.broadcasted_iota(jnp.int32, shape, dim)


def kernel(
    fresh_h, sci_h, sn_h, ngain, again, wc_h, wq_h, wk_h, wv_h, wo_h,
    out_ref,
    fresh, sci, wc, wq, wkv, wo,
    st_send, st_recv,
    colbuf, ext, xw,
    sb, kall, vx, hid,
    q_mine, q_recv, part, ret_a, lse, ret_l, st_o, st_m,
    load_sem, st_ssem, st_rsem, halo_ssem, halo_rsem,
    z_ssem, z_rsem, y_ssem, y_rsem,
    q_ssem, q_rsem, a_ssem, a_rsem, l_ssem, l_rsem,
):
    r = lax.axis_index("row")
    c = lax.axis_index("col")
    x = lax.rem(c, NX)
    ybase = c - x
    rown = [lax.rem(r + j, NZ) for j in range(NZ)]
    coln = [lax.rem(c + j, NCOL) for j in range(NCOL)]
    xn = [ybase + lax.rem(x + j, NX) for j in range(NX)]
    ypart = lax.rem(c + NX, NCOL)

    def remote(src, dst, ss, rs, dev):
        return pltpu.make_async_remote_copy(
            src_ref=src, dst_ref=dst, send_sem=ss, recv_sem=rs,
            device_id=dev, device_id_type=MESH)

    loads = [
        pltpu.make_async_copy(fresh_h, fresh, load_sem.at[0]),
        pltpu.make_async_copy(sn_h, sb.at[0, pl.ds(0, TOK)], load_sem.at[1]),
        pltpu.make_async_copy(sci_h, sci, load_sem.at[2]),
        pltpu.make_async_copy(wk_h, wkv.at[:, pl.ds(0, C)], load_sem.at[3]),
        pltpu.make_async_copy(wv_h, wkv.at[:, pl.ds(C, C)], load_sem.at[4]),
        pltpu.make_async_copy(wc_h, wc, load_sem.at[5]),
        pltpu.make_async_copy(wq_h, wq, load_sem.at[6]),
        pltpu.make_async_copy(wo_h, wo, load_sem.at[7]),
    ]
    for cp in loads:
        cp.start()

    barrier = pltpu.get_barrier_semaphore()
    partners = [{"row": rown[j]} for j in range(1, NZ)]
    partners += [{"col": coln[j]} for j in range(1, NCOL)]
    partners += [{"row": rown[i], "col": coln[j]} for i in (1, NZ - 1) for j in (1, NCOL - 1)]
    for dev in partners:
        pl.semaphore_signal(barrier, inc=1, device_id=dev, device_id_type=MESH)

    loads[0].wait()
    xf = fresh[...].astype(F32)
    s1 = jnp.sum(xf, axis=0, keepdims=True)
    s2 = jnp.sum(xf * xf, axis=0, keepdims=True)
    row8 = iota((8, C), 0)
    st = jnp.where(row8 == 0, s1, jnp.where(row8 == 1, s2, 0.0))
    per = C // GROUPS
    gc = iota((C, 128), 0)
    gl = iota((C, 128), 1) * per
    gmat = jnp.where((gc >= gl) & (gc < gl + per), 1.0, 0.0).astype(F32)
    st_send[0] = jnp.dot(st, gmat, precision=HIGH, preferred_element_type=F32)
    loads[2].wait()
    e0 = iota((16, TOK), 0)
    e1 = iota((16, TOK), 1)
    want = jnp.where(e0 < 8, e0 * PW, (e0 - 8) * PW + PW - 1)
    sel = jnp.where(e1 == want, 1.0, 0.0).astype(BF16)
    colbuf[...] = jnp.dot(sel, sci[...], preferred_element_type=F32).astype(BF16)
    loads[1].wait()

    pl.semaphore_wait(barrier, len(partners))

    def stat_copies(stage):
        devs = [{"row": rown[j]} if stage == 0 else {"col": coln[j]} for j in range(1, 8)]
        return [remote(st_send.at[stage], st_recv.at[stage, j], st_ssem.at[stage, j], st_rsem.at[stage, j], dev)
                for j, dev in enumerate(devs)]

    stat1 = stat_copies(0)
    for cp in stat1:
        cp.start()

    up, down = {"row": rown[1]}, {"row": rown[NZ - 1]}

    def ring_copy(stream, plus, step, first, rows):
        src = step - 1 if plus else (0 if step == 1 else 3 + step)
        dst = step if plus or step == 4 else 4 + step
        d = 0 if plus else 1
        return remote(sb.at[src, pl.ds(first, rows)], sb.at[dst, pl.ds(first, rows)],
                      z_ssem.at[stream, d, step - 1], z_rsem.at[stream, d, step - 1], up if plus else down)

    def y_copy(slot):
        return remote(sb.at[slot, pl.ds(64, 64)], sb.at[slot, pl.ds(TOK + 64, 64)],
                      y_ssem.at[slot], y_rsem.at[slot], {"col": ypart})

    y_first = remote(sb.at[0, pl.ds(0, 64)], sb.at[0, pl.ds(TOK, 64)],
                     y_ssem.at[8], y_rsem.at[8], {"col": ypart})
    ring = {}
    for stream in range(3):
        for step in range(1, 4):
            ring[stream, step] = [ring_copy(stream, plus, step, 64 * stream, 64) for plus in (True, False)]
    ring[0, 4] = [ring_copy(0, True, 4, 0, 64)]
    ring[1, 4] = [ring_copy(1, False, 4, 64, 64)]
    ring[2, 4] = [ring_copy(2, True, 4, TOK, 32), ring_copy(2, False, 4, TOK + 32, 32)]
    ys = {s: y_copy(s) for s in range(8)}

    def send(stream, step):
        for cp in ring[stream, step]:
            cp.start()

    def arrived(stream, step):
        for cp in ring[stream, step]:
            cp.wait_recv()

    send(0, 1)
    y_first.start()

    lft, rgt = coln[NCOL - 1], coln[1]
    upr, dnr = rown[NZ - 1], rown[1]
    top, bot = sci.at[pl.ds(0, 16)], sci.at[pl.ds(TOK - 16, 16)]
    plan = [
        (top, 144, {"row": upr}), (top, 240, {"row": upr, "col": lft}), (top, 224, {"row": upr, "col": rgt}),
        (bot, 0, {"row": dnr}), (bot, 208, {"row": dnr, "col": lft}), (bot, 192, {"row": dnr, "col": rgt}),
        (colbuf, 176, {"col": lft}), (colbuf, 160, {"col": rgt}),
    ]
    halos = [remote(src, ext.at[pl.ds(at, 16)], halo_ssem.at[i], halo_rsem.at[i], dev)
             for i, (src, at, dev) in enumerate(plan)]
    for cp in halos:
        cp.start()
    send(1, 1)
    ys[0].start()

    for p in range(PAIRS):
        vx[:, 256 * p + 128:256 * p + 256] = jnp.ones((KROWS, 128), BF16)

    def project(block, rows):
        kv = jnp.dot(block, wkv[...], preferred_element_type=F32).astype(BF16)
        for i, row in enumerate(rows):
            piece = kv[i * TOK:(i + 1) * TOK]
            kall[row:row + TOK, :] = piece[:, :C]
            for p in range(PAIRS):
                vx[row:row + TOK, 256 * p:256 * p + 128] = piece[:, C + 128 * p:C + 128 * p + 128]

    def project_blocks(*blocks):
        rows = [sb[s, 0:TOK] if far == 0 else sb[s, TOK:2 * TOK] for far, s in blocks]
        project(rows[0] if len(rows) == 1 else jnp.concatenate(rows, axis=0), [ORDER.index(k) * TOK for k in blocks])

    loads[3].wait()
    loads[4].wait()
    project_blocks((0, 0))

    tot = st_send[0]
    for j, cp in enumerate(stat1):
        cp.wait_recv()
        tot = tot + st_recv[0, j]
    st_send[1] = tot
    stat2 = stat_copies(1)
    for cp in stat2:
        cp.start()
    y_first.wait_recv()
    send(2, 1)

    pe = iota((160, 256), 0)
    ps = iota((160, 256), 1)
    pi = lax.shift_right_logical(pe, 4)
    pj = pe & 15
    inner = (pi > 0) & (pi < 9)
    vert = ((pi > 0) | (r > 0)) & ((pi < 9) | (r < NZ - 1))
    left_src = jnp.where(pj > 0, pe - 1, jnp.where(inner, 167 + pi, jnp.where(pi == 0, 207, 239)))
    right_src = jnp.where(pj < 15, pe + 1, jnp.where(inner, 175 + pi, jnp.where(pi == 0, 208, 240)))
    left_ok = vert & ((pj > 0) | (c > 0))
    right_ok = vert & ((pj < 15) | (c < NCOL - 1))
    sel_left = jnp.where(left_ok & (ps == left_src), 1.0, 0.0).astype(BF16)
    sel_right = jnp.where(right_ok & (ps == right_src), 1.0, 0.0).astype(BF16)

    arrived(0, 1)
    send(0, 2)

    tot = st_send[1]
    for j, cp in enumerate(stat2):
        cp.wait_recv()
        tot = tot + st_recv[1, j]
    count = TOK * NZ * NCOL * per
    mom = tot * (1.0 / count)
    mean_g = mom[0:1]
    var_g = mom[1:2] - mean_g * mean_g
    rstd_g = lax.rsqrt(var_g + 1e-05)
    row8 = iota((8, 128), 0)
    both = jnp.where(row8 == 0, mean_g, jnp.where(row8 == 1, rstd_g, 0.0))
    hl = iota((128, C), 0) * per
    hc = iota((128, C), 1)
    gback = jnp.where((hc >= hl) & (hc < hl + per), 1.0, 0.0).astype(F32)
    wide = jnp.dot(both, gback, precision=HIGH, preferred_element_type=F32)
    xf = fresh[...].astype(F32)
    v = (xf - wide[0:1]) * wide[1:2] * ngain[...].reshape(1, C)
    ext[16:16 + TOK, :] = (v * (1.0 / (1.0 + jnp.exp(-v)))).astype(BF16)
    arrived(1, 1)
    send(1, 2)
    ys[1].start()
    ys[5].start()
    for cp in halos:
        cp.wait_recv()
    zero = jnp.zeros((16, C), BF16)
    ext[0:16, :] = jnp.where(r > 0, ext[0:16, :], zero)
    ext[144:160, :] = jnp.where(r < NZ - 1, ext[144:160, :], zero)
    whole = ext[...]
    e_left = jnp.dot(sel_left, whole, preferred_element_type=F32).astype(BF16)
    e_right = jnp.dot(sel_right, whole, preferred_element_type=F32).astype(BF16)
    for a in range(3):
        xw[:, (3 * a) * C:(3 * a + 1) * C] = e_left[16 * a:16 * a + TOK]
        xw[:, (3 * a + 1) * C:(3 * a + 2) * C] = ext[16 * a:16 * a + TOK, :]
        xw[:, (3 * a + 2) * C:(3 * a + 3) * C] = e_right[16 * a:16 * a + TOK]
    loads[5].wait()
    hidden = xf + jnp.dot(xw[...], wc[...], preferred_element_type=F32)
    hid[...] = hidden
    mean = jnp.mean(hidden, axis=-1, keepdims=True)
    cen = hidden - mean
    var = jnp.mean(cen * cen, axis=-1, keepdims=True)
    normed = (cen * lax.rsqrt(var + 1e-05) * again[...].reshape(1, C)).astype(BF16)
    loads[6].wait()
    q_mine[...] = (jnp.dot(normed, wq[...], preferred_element_type=F32) * (LOG2E / 8)).astype(BF16)
    q_cp = {j: remote(q_mine, q_recv.at[NX - j - 1], q_ssem.at[j - 1], q_rsem.at[NX - j - 1], {"col": xn[j]})
            for j in (1, 3, 2)}
    for cp in q_cp.values():
        cp.start()
    project(normed, [0])

    lane = iota((TOK, 128), 1)

    def attend(slot, first, base, span, final):
        q_ref = q_mine if slot == 0 else q_recv.at[slot - 1]
        table = jnp.zeros((TOK, 128), F32)
        for p in range(PAIRS):
            qp = q_ref[:, 128 * p:128 * p + 128]
            zq = jnp.zeros_like(qp)
            qm = jnp.concatenate([jnp.where(lane < HEAD, qp, zq), jnp.where(lane < HEAD, zq, qp)], axis=0)
            s = lax.dot_general(qm, kall[base:base + span, 128 * p:128 * p + 128], NT, preferred_element_type=F32)
            m = jnp.max(s, axis=1, keepdims=True)
            if not first:
                before = st_m[slot, p][:, :1]
                m = jnp.maximum(m, before)
            w = jnp.exp2(s - m).astype(BF16)
            o = jnp.dot(w, vx[base:base + span, 256 * p:256 * p + 256], preferred_element_type=F32)
            if not first:
                o = o + st_o[slot, p] * jnp.exp2(before - m)
            if not final:
                st_m[slot, p] = jnp.broadcast_to(m, (2 * TOK, 128))
                st_o[slot, p] = o
                continue
            den = o[:, 128:]
            norm = o[:, :128] / den
            part[slot, :, 128 * p:128 * p + 128] = jnp.where(lane < HEAD, norm[:TOK], norm[TOK:]).astype(BF16)
            ls = m + jnp.log2(den)
            table = jnp.where(lane == 2 * p, ls[:TOK], jnp.where(lane == 2 * p + 1, ls[TOK:], table))
        if final:
            lse[slot] = table.T[:16]

    def attend_a(slot):
        attend(slot, True, 0 if slot == 0 else TOK, 8 * TOK, False)

    def attend_b(slot):
        attend(slot, False, 9 * TOK, 4 * TOK, False)

    def attend_c(slot):
        attend(slot, False, 13 * TOK, 4 * TOK, True)

    arrived(2, 1)
    send(2, 2)
    arrived(0, 2)
    send(0, 3)
    project_blocks((0, 1), (0, 5))
    arrived(1, 2)
    send(1, 3)
    ys[2].start()
    ys[6].start()
    project_blocks((0, 2), (0, 6))
    for s in (0, 1, 5):
        ys[s].wait_recv()
    project_blocks((1, 0), (1, 1), (1, 5))
    attend_a(0)
    arrived(0, 3)
    send(0, 4)
    arrived(2, 2)
    send(2, 3)
    arrived(1, 3)
    send(1, 4)
    ys[3].start()
    ys[7].start()
    project_blocks((0, 3), (0, 7))
    for s in (2, 6):
        ys[s].wait_recv()
    project_blocks((1, 2), (1, 6))
    q_cp[NX - 1].wait_recv()
    attend_a(1)
    arrived(2, 3)
    send(2, 4)
    q_cp[NX - 3].wait_recv()
    attend_a(3)
    arrived(0, 4)
    arrived(1, 4)
    ys[4].start()
    attend_b(1)
    attend_b(3)
    q_cp[NX - 2].wait_recv()
    attend_a(2)
    attend_b(2)
    for s in (3, 7):
        ys[s].wait_recv()
    project_blocks((0, 4), (1, 3), (1, 7))
    arrived(2, 4)
    ys[4].wait_recv()
    project_blocks((1, 4))
    backs = []
    for j in (2, 1, 3):
        attend_c(j)
        dst = NX - j - 1
        a_cp = remote(part.at[j], ret_a.at[dst], a_ssem.at[j - 1], a_rsem.at[dst], {"col": xn[j]})
        l_cp = remote(lse.at[j], ret_l.at[dst], l_ssem.at[j - 1], l_rsem.at[dst], {"col": xn[j]})
        a_cp.start()
        l_cp.start()
        backs += [a_cp, l_cp]
    attend_b(0)
    attend_c(0)
    for cp in backs:
        cp.wait_recv()

    ls = [lse[0]] + [ret_l[j] for j in range(3)]
    top_l = jnp.maximum(jnp.maximum(ls[0], ls[1]), jnp.maximum(ls[2], ls[3]))
    ws = [jnp.exp2(l - top_l) for l in ls]
    inv = 1.0 / (ws[0] + ws[1] + ws[2] + ws[3])
    eh = iota((32, C), 0) & 15
    ec = iota((32, C), 1)
    spread = jnp.where((ec >= eh * HEAD) & (ec < eh * HEAD + HEAD), 1.0, 0.0).astype(BF16)
    att = jnp.zeros((TOK, C), F32)
    for i in range(4):
        share = ws[i] * inv
        hi = share.astype(BF16)
        lo = (share - hi.astype(F32)).astype(BF16)
        split = jnp.concatenate([hi, lo], axis=0)
        full = lax.dot_general(split, spread, TN, preferred_element_type=F32)
        val = part[0] if i == 0 else ret_a[i - 1]
        att = att + full * val.astype(F32)
    loads[7].wait()
    out = hid[...] + jnp.dot(att.astype(BF16), wo[...], preferred_element_type=F32)
    out_ref[...] = out.astype(BF16)

    sends = stat1 + stat2 + halos + [y_first] + [cp for some in ring.values() for cp in some]
    sends += list(ys.values()) + list(q_cp.values()) + backs
    for cp in sends:
        cp.wait_send()


def on_device(fresh, stale_conv_in, stale_normed, norm_gain, conv_weight, attn_gain, w_query, w_key, w_value, w_out):
    shape = fresh.shape
    flat = lambda a: a.reshape(TOK, C)
    hbm = pl.BlockSpec(memory_space=pl.ANY)
    vmem = pl.BlockSpec(memory_space=pltpu.VMEM)
    dma = pltpu.SemaphoreType.DMA
    V = pltpu.VMEM
    out = pl.pallas_call(
        kernel,
        out_shape=jax.ShapeDtypeStruct((TOK, C), BF16),
        in_specs=[hbm] * 3 + [vmem] * 2 + [hbm] * 5,
        out_specs=vmem,
        scratch_shapes=[
            V((TOK, C), BF16), V((TOK, C), BF16), V((9 * C, C), BF16), V((C, C), BF16), V((C, 2 * C), BF16), V((C, C), BF16),
            V((2, 8, 128), F32), V((2, 7, 8, 128), F32),
            V((16, C), BF16), V((256, C), BF16), V((TOK, 9 * C), BF16),
            V((NZ, 2 * TOK, C), BF16), V((KROWS, C), BF16), V((KROWS, 256 * PAIRS), BF16), V((TOK, C), F32),
            V((TOK, C), BF16), V((3, TOK, C), BF16), V((4, TOK, C), BF16), V((3, TOK, C), BF16),
            V((4, 16, 128), F32), V((3, 16, 128), F32),
            V((4, PAIRS, 2 * TOK, 256), F32), V((4, PAIRS, 2 * TOK, 128), F32),
            dma((8,)), dma((2, 7)), dma((2, 7)), dma((8,)), dma((8,)),
            dma((3, 2, 4)), dma((3, 2, 4)), dma((9,)), dma((9,)),
            dma((3,)), dma((3,)), dma((3,)), dma((3,)), dma((3,)), dma((3,)),
        ],
        compiler_params=pltpu.CompilerParams(
            collective_id=0, has_side_effects=True, vmem_limit_bytes=60 * 2**20),
    )(
        flat(fresh), flat(stale_conv_in), flat(stale_normed),
        norm_gain, attn_gain,
        conv_weight.reshape(9 * C, C), w_query, w_key, w_value, w_out,
    )
    return out.reshape(shape)


def solution(mesh):
    cells = P(("img", "row"), "col", None)
    return jax.shard_map(
        on_device,
        mesh=mesh,
        in_specs=(cells, cells, cells) + (P(),) * 7,
        out_specs=cells,
        check_vma=False,
    )
```

```python
import functools
import jax
import jax.numpy as jnp
from jax import lax
from jax.experimental import pallas as pl
from jax.experimental.pallas import tpu as pltpu
from jax.sharding import PartitionSpec as P

GROUPS = 32
HEAD = 64
C = 640
TOK = 128
PW = 16
NZ = 8
NX = 4
NCOL = 8
PAIRS = 5
KROWS = 17 * TOK
ORDER = [None, (0, 1), (0, 5), (0, 2), (0, 6), (1, 0), (1, 1), (1, 5), (0, 0),
         (0, 3), (0, 7), (1, 2), (1, 6), (0, 4), (1, 3), (1, 7), (1, 4)]
LOG2E = 1.4426950408889634
MESH = pl.DeviceIdType.MESH
F32 = jnp.float32
BF16 = jnp.bfloat16
HIGH = lax.Precision.HIGHEST
NT = (((1,), (1,)), ((), ()))
TN = (((0,), (0,)), ((), ()))


def iota(shape, dim):
    return lax.broadcasted_iota(jnp.int32, shape, dim)


def kernel(
    fresh_h, sci_h, sn_h, ngain, again, wc_h, wq_h, wk_h, wv_h, wo_h,
    out_ref,
    fresh, sci, wc, wq, wkv, wo,
    st_send, st_recv,
    colbuf, ext, xw,
    sb, kall, vx, hid,
    q_mine, q_recv, part, ret_a, lse, ret_l, st_o, st_m,
    load_sem, st_ssem, st_rsem, halo_ssem, halo_rsem,
    z_ssem, z_rsem, y_ssem, y_rsem,
    q_ssem, q_rsem, a_ssem, a_rsem, l_ssem, l_rsem,
):
    r = lax.axis_index("row")
    c = lax.axis_index("col")
    x = lax.rem(c, NX)
    ybase = c - x
    rown = [lax.rem(r + j, NZ) for j in range(NZ)]
    coln = [lax.rem(c + j, NCOL) for j in range(NCOL)]
    xn = [ybase + lax.rem(x + j, NX) for j in range(NX)]
    ypart = lax.rem(c + NX, NCOL)

    def remote(src, dst, ss, rs, dev):
        return pltpu.make_async_remote_copy(
            src_ref=src, dst_ref=dst, send_sem=ss, recv_sem=rs,
            device_id=dev, device_id_type=MESH)

    loads = [
        pltpu.make_async_copy(fresh_h, fresh, load_sem.at[0]),
        pltpu.make_async_copy(sn_h, sb.at[0, pl.ds(0, TOK)], load_sem.at[1]),
        pltpu.make_async_copy(sci_h, sci, load_sem.at[2]),
        pltpu.make_async_copy(wk_h, wkv.at[:, pl.ds(0, C)], load_sem.at[3]),
        pltpu.make_async_copy(wv_h, wkv.at[:, pl.ds(C, C)], load_sem.at[4]),
        pltpu.make_async_copy(wc_h, wc, load_sem.at[5]),
        pltpu.make_async_copy(wq_h, wq, load_sem.at[6]),
        pltpu.make_async_copy(wo_h, wo, load_sem.at[7]),
    ]
    for cp in loads:
        cp.start()

    barrier = pltpu.get_barrier_semaphore()
    partners = [{"row": rown[j]} for j in range(1, NZ)]
    partners += [{"col": coln[j]} for j in range(1, NCOL)]
    partners += [{"row": rown[i], "col": coln[j]} for i in (1, NZ - 1) for j in (1, NCOL - 1)]
    for dev in partners:
        pl.semaphore_signal(barrier, inc=1, device_id=dev, device_id_type=MESH)

    loads[0].wait()
    xf = fresh[...].astype(F32)
    s1 = jnp.sum(xf, axis=0, keepdims=True)
    s2 = jnp.sum(xf * xf, axis=0, keepdims=True)
    row8 = iota((8, C), 0)
    st = jnp.where(row8 == 0, s1, jnp.where(row8 == 1, s2, 0.0))
    per = C // GROUPS
    gc = iota((C, 128), 0)
    gl = iota((C, 128), 1) * per
    gmat = jnp.where((gc >= gl) & (gc < gl + per), 1.0, 0.0).astype(F32)
    st_send[0] = jnp.dot(st, gmat, precision=HIGH, preferred_element_type=F32)
    loads[2].wait()
    e0 = iota((16, TOK), 0)
    e1 = iota((16, TOK), 1)
    want = jnp.where(e0 < 8, e0 * PW, (e0 - 8) * PW + PW - 1)
    sel = jnp.where(e1 == want, 1.0, 0.0).astype(BF16)
    colbuf[...] = jnp.dot(sel, sci[...], preferred_element_type=F32).astype(BF16)
    loads[1].wait()

    pl.semaphore_wait(barrier, len(partners))

    def stat_copies(stage):
        devs = [{"row": rown[j]} if stage == 0 else {"col": coln[j]} for j in range(1, 8)]
        return [remote(st_send.at[stage], st_recv.at[stage, j], st_ssem.at[stage, j], st_rsem.at[stage, j], dev)
                for j, dev in enumerate(devs)]

    stat1 = stat_copies(0)
    for cp in stat1:
        cp.start()

    up, down = {"row": rown[1]}, {"row": rown[NZ - 1]}

    def ring_copy(stream, plus, step, first, rows):
        src = step - 1 if plus else (0 if step == 1 else 3 + step)
        dst = step if plus or step == 4 else 4 + step
        d = 0 if plus else 1
        return remote(sb.at[src, pl.ds(first, rows)], sb.at[dst, pl.ds(first, rows)],
                      z_ssem.at[stream, d, step - 1], z_rsem.at[stream, d, step - 1], up if plus else down)

    def y_copy(slot):
        return remote(sb.at[slot, pl.ds(64, 64)], sb.at[slot, pl.ds(TOK + 64, 64)],
                      y_ssem.at[slot], y_rsem.at[slot], {"col": ypart})

    y_first = remote(sb.at[0, pl.ds(0, 64)], sb.at[0, pl.ds(TOK, 64)],
                     y_ssem.at[8], y_rsem.at[8], {"col": ypart})
    ring = {}
    for stream in range(3):
        for step in range(1, 4):
            ring[stream, step] = [ring_copy(stream, plus, step, 64 * stream, 64) for plus in (True, False)]
    ring[0, 4] = [ring_copy(0, True, 4, 0, 64)]
    ring[1, 4] = [ring_copy(1, False, 4, 64, 64)]
    ring[2, 4] = [ring_copy(2, True, 4, TOK, 32), ring_copy(2, False, 4, TOK + 32, 32)]
    ys = {s: y_copy(s) for s in range(8)}

    def send(stream, step):
        for cp in ring[stream, step]:
            cp.start()

    def arrived(stream, step):
        for cp in ring[stream, step]:
            cp.wait_recv()

    send(1, 1)
    y_first.start()

    lft, rgt = coln[NCOL - 1], coln[1]
    upr, dnr = rown[NZ - 1], rown[1]
    top, bot = sci.at[pl.ds(0, 16)], sci.at[pl.ds(TOK - 16, 16)]
    plan = [
        (top, 144, {"row": upr}), (top, 240, {"row": upr, "col": lft}), (top, 224, {"row": upr, "col": rgt}),
        (bot, 0, {"row": dnr}), (bot, 208, {"row": dnr, "col": lft}), (bot, 192, {"row": dnr, "col": rgt}),
        (colbuf, 176, {"col": lft}), (colbuf, 160, {"col": rgt}),
    ]
    halos = [remote(src, ext.at[pl.ds(at, 16)], halo_ssem.at[i], halo_rsem.at[i], dev)
             for i, (src, at, dev) in enumerate(plan)]
    for cp in halos:
        cp.start()
    send(0, 1)
    ys[0].start()

    for p in range(PAIRS):
        vx[:, 256 * p + 128:256 * p + 256] = jnp.ones((KROWS, 128), BF16)

    def project(block, rows):
        kv = jnp.dot(block, wkv[...], preferred_element_type=F32).astype(BF16)
        for i, row in enumerate(rows):
            piece = kv[i * TOK:(i + 1) * TOK]
            kall[row:row + TOK, :] = piece[:, :C]
            for p in range(PAIRS):
                vx[row:row + TOK, 256 * p:256 * p + 128] = piece[:, C + 128 * p:C + 128 * p + 128]

    def project_blocks(*blocks):
        rows = [sb[s, 0:TOK] if far == 0 else sb[s, TOK:2 * TOK] for far, s in blocks]
        project(rows[0] if len(rows) == 1 else jnp.concatenate(rows, axis=0), [ORDER.index(k) * TOK for k in blocks])

    loads[3].wait()
    loads[4].wait()
    project_blocks((0, 0))

    tot = st_send[0]
    for j, cp in enumerate(stat1):
        cp.wait_recv()
        tot = tot + st_recv[0, j]
    st_send[1] = tot
    stat2 = stat_copies(1)
    for cp in stat2:
        cp.start()
    y_first.wait_recv()
    send(2, 1)

    pe = iota((160, 256), 0)
    ps = iota((160, 256), 1)
    pi = lax.shift_right_logical(pe, 4)
    pj = pe & 15
    inner = (pi > 0) & (pi < 9)
    vert = ((pi > 0) | (r > 0)) & ((pi < 9) | (r < NZ - 1))
    left_src = jnp.where(pj > 0, pe - 1, jnp.where(inner, 167 + pi, jnp.where(pi == 0, 207, 239)))
    right_src = jnp.where(pj < 15, pe + 1, jnp.where(inner, 175 + pi, jnp.where(pi == 0, 208, 240)))
    left_ok = vert & ((pj > 0) | (c > 0))
    right_ok = vert & ((pj < 15) | (c < NCOL - 1))
    sel_left = jnp.where(left_ok & (ps == left_src), 1.0, 0.0).astype(BF16)
    sel_right = jnp.where(right_ok & (ps == right_src), 1.0, 0.0).astype(BF16)

    arrived(1, 1)
    send(1, 2)
    ys[1].start()
    ys[5].start()
    arrived(0, 1)
    send(0, 2)

    tot = st_send[1]
    for j, cp in enumerate(stat2):
        cp.wait_recv()
        tot = tot + st_recv[1, j]
    count = TOK * NZ * NCOL * per
    mom = tot * (1.0 / count)
    mean_g = mom[0:1]
    var_g = mom[1:2] - mean_g * mean_g
    rstd_g = lax.rsqrt(var_g + 1e-05)
    row8 = iota((8, 128), 0)
    both = jnp.where(row8 == 0, mean_g, jnp.where(row8 == 1, rstd_g, 0.0))
    hl = iota((128, C), 0) * per
    hc = iota((128, C), 1)
    gback = jnp.where((hc >= hl) & (hc < hl + per), 1.0, 0.0).astype(F32)
    wide = jnp.dot(both, gback, precision=HIGH, preferred_element_type=F32)
    xf = fresh[...].astype(F32)
    v = (xf - wide[0:1]) * wide[1:2] * ngain[...].reshape(1, C)
    ext[16:16 + TOK, :] = (v * (1.0 / (1.0 + jnp.exp(-v)))).astype(BF16)
    for cp in halos:
        cp.wait_recv()
    zero = jnp.zeros((16, C), BF16)
    ext[0:16, :] = jnp.where(r > 0, ext[0:16, :], zero)
    ext[144:160, :] = jnp.where(r < NZ - 1, ext[144:160, :], zero)
    whole = ext[...]
    e_left = jnp.dot(sel_left, whole, preferred_element_type=F32).astype(BF16)
    e_right = jnp.dot(sel_right, whole, preferred_element_type=F32).astype(BF16)
    for a in range(3):
        xw[:, (3 * a) * C:(3 * a + 1) * C] = e_left[16 * a:16 * a + TOK]
        xw[:, (3 * a + 1) * C:(3 * a + 2) * C] = ext[16 * a:16 * a + TOK, :]
        xw[:, (3 * a + 2) * C:(3 * a + 3) * C] = e_right[16 * a:16 * a + TOK]
    loads[5].wait()
    hidden = xf + jnp.dot(xw[...], wc[...], preferred_element_type=F32)
    hid[...] = hidden
    mean = jnp.mean(hidden, axis=-1, keepdims=True)
    cen = hidden - mean
    var = jnp.mean(cen * cen, axis=-1, keepdims=True)
    normed = (cen * lax.rsqrt(var + 1e-05) * again[...].reshape(1, C)).astype(BF16)
    loads[6].wait()
    q_mine[...] = (jnp.dot(normed, wq[...], preferred_element_type=F32) * (LOG2E / 8)).astype(BF16)
    q_cp = {j: remote(q_mine, q_recv.at[NX - j - 1], q_ssem.at[j - 1], q_rsem.at[NX - j - 1], {"col": xn[j]})
            for j in (1, 3, 2)}
    q_cp[1].start()
    q_cp[3].start()
    arrived(1, 2)
    send(1, 3)
    ys[2].start()
    ys[6].start()
    arrived(0, 2)
    send(0, 3)
    arrived(2, 1)
    send(2, 2)
    q_cp[2].start()
    project(normed, [0])

    lane = iota((TOK, 128), 1)

    def attend(slot, base, span, pairs=range(PAIRS), first=True, final=False, table=None):
        q_ref = q_mine if slot == 0 else q_recv.at[slot - 1]
        if table is None:
            table = jnp.zeros((TOK, 128), F32)
        for p in pairs:
            qp = q_ref[:, 128 * p:128 * p + 128]
            zq = jnp.zeros_like(qp)
            qm = jnp.concatenate([jnp.where(lane < HEAD, qp, zq), jnp.where(lane < HEAD, zq, qp)], axis=0)
            s = lax.dot_general(qm, kall[base:base + span, 128 * p:128 * p + 128], NT, preferred_element_type=F32)
            m = jnp.max(s, axis=1, keepdims=True)
            if not first:
                before = st_m[slot, p][:, :1]
                m = jnp.maximum(m, before)
            w = jnp.exp2(s - m).astype(BF16)
            o = jnp.dot(w, vx[base:base + span, 256 * p:256 * p + 256], preferred_element_type=F32)
            if not first:
                o = o + st_o[slot, p] * jnp.exp2(before - m)
            if not final:
                st_m[slot, p] = jnp.broadcast_to(m, (2 * TOK, 128))
                st_o[slot, p] = o
                continue
            den = o[:, 128:]
            norm = o[:, :128] / den
            part[slot, :, 128 * p:128 * p + 128] = jnp.where(lane < HEAD, norm[:TOK], norm[TOK:]).astype(BF16)
            ls = m + jnp.log2(den)
            table = jnp.where(lane == 2 * p, ls[:TOK], jnp.where(lane == 2 * p + 1, ls[TOK:], table))
        if final:
            lse[slot] = table.T[:16]
        return table

    project_blocks((0, 1), (0, 5), (0, 2), (0, 6))
    for s in (0, 1, 5):
        ys[s].wait_recv()
    project_blocks((1, 0), (1, 1), (1, 5))
    attend(0, 0, 8 * TOK)
    arrived(1, 3)
    send(1, 4)
    ys[3].start()
    ys[7].start()
    arrived(0, 3)
    send(0, 4)
    arrived(2, 2)
    send(2, 3)
    ys[2].wait_recv()
    ys[6].wait_recv()
    project_blocks((0, 3), (0, 7), (1, 2), (1, 6))
    q_cp[NX - 1].wait_recv()
    attend(1, TOK, 12 * TOK)
    arrived(1, 4)
    ys[4].start()
    arrived(0, 4)
    arrived(2, 3)
    send(2, 4)
    ys[3].wait_recv()
    ys[7].wait_recv()
    project_blocks((0, 4), (1, 3), (1, 7))
    q_cp[NX - 3].wait_recv()
    attend(3, TOK, 12 * TOK)
    arrived(2, 4)
    ys[4].wait_recv()
    project_blocks((1, 4))
    backs = []

    def give_back(j, g, at, wide_g):
        dst = NX - j - 1
        cp = remote(part.at[j, :, pl.ds(at, wide_g)], ret_a.at[dst, :, pl.ds(at, wide_g)],
                    a_ssem.at[j - 1, g], a_rsem.at[dst, g], {"col": xn[j]})
        cp.start()
        backs.append(cp)

    def give_lse(j):
        dst = NX - j - 1
        cp = remote(lse.at[j], ret_l.at[dst], l_ssem.at[j - 1], l_rsem.at[dst], {"col": xn[j]})
        cp.start()
        backs.append(cp)

    for j in (1, 3):
        attend(j, 13 * TOK, 4 * TOK, first=False, final=True)
        give_back(j, 0, 0, C)
        give_lse(j)
    q_cp[NX - 2].wait_recv()
    table = attend(2, TOK, 16 * TOK, range(0, 3), final=True)
    give_back(2, 0, 0, 384)
    attend(2, TOK, 16 * TOK, range(3, PAIRS), final=True, table=table)
    give_back(2, 1, 384, 256)
    give_lse(2)
    attend(0, 9 * TOK, 8 * TOK, first=False, final=True)
    for cp in backs:
        cp.wait_recv()

    ls = [lse[0]] + [ret_l[j] for j in range(3)]
    top_l = jnp.maximum(jnp.maximum(ls[0], ls[1]), jnp.maximum(ls[2], ls[3]))
    ws = [jnp.exp2(l - top_l) for l in ls]
    inv = 1.0 / (ws[0] + ws[1] + ws[2] + ws[3])
    eh = iota((32, C), 0) & 15
    ec = iota((32, C), 1)
    spread = jnp.where((ec >= eh * HEAD) & (ec < eh * HEAD + HEAD), 1.0, 0.0).astype(BF16)
    att = jnp.zeros((TOK, C), F32)
    for i in range(4):
        share = ws[i] * inv
        hi = share.astype(BF16)
        lo = (share - hi.astype(F32)).astype(BF16)
        split = jnp.concatenate([hi, lo], axis=0)
        full = lax.dot_general(split, spread, TN, preferred_element_type=F32)
        val = part[0] if i == 0 else ret_a[i - 1]
        att = att + full * val.astype(F32)
    loads[7].wait()
    out = hid[...] + jnp.dot(att.astype(BF16), wo[...], preferred_element_type=F32)
    out_ref[...] = out.astype(BF16)

    sends = stat1 + stat2 + halos + [y_first] + [cp for some in ring.values() for cp in some]
    sends += list(ys.values()) + list(q_cp.values()) + backs
    for cp in sends:
        cp.wait_send()


def on_device(fresh, stale_conv_in, stale_normed, norm_gain, conv_weight, attn_gain, w_query, w_key, w_value, w_out):
    shape = fresh.shape
    flat = lambda a: a.reshape(TOK, C)
    hbm = pl.BlockSpec(memory_space=pl.ANY)
    vmem = pl.BlockSpec(memory_space=pltpu.VMEM)
    dma = pltpu.SemaphoreType.DMA
    V = pltpu.VMEM
    out = pl.pallas_call(
        kernel,
        out_shape=jax.ShapeDtypeStruct((TOK, C), BF16),
        in_specs=[hbm] * 3 + [vmem] * 2 + [hbm] * 5,
        out_specs=vmem,
        scratch_shapes=[
            V((TOK, C), BF16), V((TOK, C), BF16), V((9 * C, C), BF16), V((C, C), BF16), V((C, 2 * C), BF16), V((C, C), BF16),
            V((2, 8, 128), F32), V((2, 7, 8, 128), F32),
            V((16, C), BF16), V((256, C), BF16), V((TOK, 9 * C), BF16),
            V((NZ, 2 * TOK, C), BF16), V((KROWS, C), BF16), V((KROWS, 256 * PAIRS), BF16), V((TOK, C), F32),
            V((TOK, C), BF16), V((3, TOK, C), BF16), V((4, TOK, C), BF16), V((3, TOK, C), BF16),
            V((4, 16, 128), F32), V((3, 16, 128), F32),
            V((4, PAIRS, 2 * TOK, 256), F32), V((4, PAIRS, 2 * TOK, 128), F32),
            dma((8,)), dma((2, 7)), dma((2, 7)), dma((8,)), dma((8,)),
            dma((3, 2, 4)), dma((3, 2, 4)), dma((9,)), dma((9,)),
            dma((3,)), dma((3,)), dma((3, 2)), dma((3, 2)), dma((3,)), dma((3,)),
        ],
        compiler_params=pltpu.CompilerParams(
            collective_id=0, has_side_effects=True, vmem_limit_bytes=60 * 2**20),
    )(
        flat(fresh), flat(stale_conv_in), flat(stale_normed),
        norm_gain, attn_gain,
        conv_weight.reshape(9 * C, C), w_query, w_key, w_value, w_out,
    )
    return out.reshape(shape)


def solution(mesh):
    cells = P(("img", "row"), "col", None)
    return jax.shard_map(
        on_device,
        mesh=mesh,
        in_specs=(cells, cells, cells) + (P(),) * 7,
        out_specs=cells,
        check_vma=False,
    )
```

```python
import functools
import jax
import jax.numpy as jnp
from jax import lax
from jax.experimental import pallas as pl
from jax.experimental.pallas import tpu as pltpu
from jax.sharding import PartitionSpec as P

GROUPS = 32
HEAD = 64
C = 640
TOK = 128
PW = 16
NZ = 8
NX = 4
NCOL = 8
PAIRS = 5
KROWS = 17 * TOK
ORDER = [None, (0, 1), (0, 5), (0, 2), (0, 6), (1, 0), (1, 1), (1, 5), (0, 0),
         (0, 3), (0, 7), (1, 2), (1, 6), (0, 4), (1, 3), (1, 7), (1, 4)]
LOG2E = 1.4426950408889634
MESH = pl.DeviceIdType.MESH
F32 = jnp.float32
BF16 = jnp.bfloat16
HIGH = lax.Precision.HIGHEST
NT = (((1,), (1,)), ((), ()))
TN = (((0,), (0,)), ((), ()))


def iota(shape, dim):
    return lax.broadcasted_iota(jnp.int32, shape, dim)


def kernel(
    fresh_h, sci_h, sn_h, ngain, again, wc_h, wq_h, wk_h, wv_h, wo_h,
    out_ref,
    fresh, sci, wc, wq, wkv, wo,
    st_send, st_recv,
    colbuf, ext, xw,
    sb, kall, vx, hid,
    q_mine, q_recv, part, ret_a, lse, ret_l, st_o, st_m,
    load_sem, st_ssem, st_rsem, halo_ssem, halo_rsem,
    z_ssem, z_rsem, y_ssem, y_rsem,
    q_ssem, q_rsem, a_ssem, a_rsem, l_ssem, l_rsem,
):
    r = lax.axis_index("row")
    c = lax.axis_index("col")
    x = lax.rem(c, NX)
    ybase = c - x
    rown = [lax.rem(r + j, NZ) for j in range(NZ)]
    coln = [lax.rem(c + j, NCOL) for j in range(NCOL)]
    xn = [ybase + lax.rem(x + j, NX) for j in range(NX)]
    ypart = lax.rem(c + NX, NCOL)

    def remote(src, dst, ss, rs, dev):
        return pltpu.make_async_remote_copy(
            src_ref=src, dst_ref=dst, send_sem=ss, recv_sem=rs,
            device_id=dev, device_id_type=MESH)

    loads = [
        pltpu.make_async_copy(fresh_h, fresh, load_sem.at[0]),
        pltpu.make_async_copy(sn_h, sb.at[0, pl.ds(0, TOK)], load_sem.at[1]),
        pltpu.make_async_copy(sci_h, sci, load_sem.at[2]),
        pltpu.make_async_copy(wk_h, wkv.at[:, pl.ds(0, C)], load_sem.at[3]),
        pltpu.make_async_copy(wv_h, wkv.at[:, pl.ds(C, C)], load_sem.at[4]),
        pltpu.make_async_copy(wc_h, wc, load_sem.at[5]),
        pltpu.make_async_copy(wq_h, wq, load_sem.at[6]),
        pltpu.make_async_copy(wo_h, wo, load_sem.at[7]),
    ]
    for cp in loads:
        cp.start()

    barrier = pltpu.get_barrier_semaphore()
    partners = [{"row": rown[j]} for j in range(1, NZ)]
    partners += [{"col": coln[j]} for j in range(1, NCOL)]
    partners += [{"row": rown[i], "col": coln[j]} for i in (1, NZ - 1) for j in (1, NCOL - 1)]
    for dev in partners:
        pl.semaphore_signal(barrier, inc=1, device_id=dev, device_id_type=MESH)

    loads[0].wait()
    xf = fresh[...].astype(F32)
    s1 = jnp.sum(xf, axis=0, keepdims=True)
    s2 = jnp.sum(xf * xf, axis=0, keepdims=True)
    row8 = iota((8, C), 0)
    st = jnp.where(row8 == 0, s1, jnp.where(row8 == 1, s2, 0.0))
    per = C // GROUPS
    gc = iota((C, 128), 0)
    gl = iota((C, 128), 1) * per
    gmat = jnp.where((gc >= gl) & (gc < gl + per), 1.0, 0.0).astype(F32)
    st_send[0] = jnp.dot(st, gmat, precision=HIGH, preferred_element_type=F32)
    loads[2].wait()
    e0 = iota((16, TOK), 0)
    e1 = iota((16, TOK), 1)
    want = jnp.where(e0 < 8, e0 * PW, (e0 - 8) * PW + PW - 1)
    sel = jnp.where(e1 == want, 1.0, 0.0).astype(BF16)
    colbuf[...] = jnp.dot(sel, sci[...], preferred_element_type=F32).astype(BF16)
    loads[1].wait()

    pl.semaphore_wait(barrier, len(partners))

    def stat_copies(stage):
        devs = [{"row": rown[j]} if stage == 0 else {"col": coln[j]} for j in range(1, 8)]
        return [remote(st_send.at[stage], st_recv.at[stage, j], st_ssem.at[stage, j], st_rsem.at[stage, j], dev)
                for j, dev in enumerate(devs)]

    stat1 = stat_copies(0)
    for cp in stat1:
        cp.start()

    up, down = {"row": rown[1]}, {"row": rown[NZ - 1]}

    def ring_copy(stream, plus, step, first, rows):
        src = step - 1 if plus else (0 if step == 1 else 3 + step)
        dst = step if plus or step == 4 else 4 + step
        d = 0 if plus else 1
        return remote(sb.at[src, pl.ds(first, rows)], sb.at[dst, pl.ds(first, rows)],
                      z_ssem.at[stream, d, step - 1], z_rsem.at[stream, d, step - 1], up if plus else down)

    def y_copy(slot):
        return remote(sb.at[slot, pl.ds(64, 64)], sb.at[slot, pl.ds(TOK + 64, 64)],
                      y_ssem.at[slot], y_rsem.at[slot], {"col": ypart})

    y_first = remote(sb.at[0, pl.ds(0, 64)], sb.at[0, pl.ds(TOK, 64)],
                     y_ssem.at[8], y_rsem.at[8], {"col": ypart})
    ring = {}
    for stream in range(3):
        for step in range(1, 4):
            ring[stream, step] = [ring_copy(stream, plus, step, 64 * stream, 64) for plus in (True, False)]
    ring[0, 4] = [ring_copy(0, True, 4, 0, 64)]
    ring[1, 4] = [ring_copy(1, False, 4, 64, 64)]
    ring[2, 4] = [ring_copy(2, True, 4, TOK, 32), ring_copy(2, False, 4, TOK + 32, 32)]
    ys = {s: y_copy(s) for s in range(8)}

    def send(stream, step):
        for cp in ring[stream, step]:
            cp.start()

    def arrived(stream, step):
        for cp in ring[stream, step]:
            cp.wait_recv()

    send(1, 1)
    y_first.start()

    lft, rgt = coln[NCOL - 1], coln[1]
    upr, dnr = rown[NZ - 1], rown[1]
    top, bot = sci.at[pl.ds(0, 16)], sci.at[pl.ds(TOK - 16, 16)]
    plan = [
        (top, 144, {"row": upr}), (top, 240, {"row": upr, "col": lft}), (top, 224, {"row": upr, "col": rgt}),
        (bot, 0, {"row": dnr}), (bot, 208, {"row": dnr, "col": lft}), (bot, 192, {"row": dnr, "col": rgt}),
        (colbuf, 176, {"col": lft}), (colbuf, 160, {"col": rgt}),
    ]
    halos = [remote(src, ext.at[pl.ds(at, 16)], halo_ssem.at[i], halo_rsem.at[i], dev)
             for i, (src, at, dev) in enumerate(plan)]
    for cp in halos:
        cp.start()
    send(0, 1)
    ys[0].start()

    for p in range(PAIRS):
        vx[:, 256 * p + 128:256 * p + 256] = jnp.ones((KROWS, 128), BF16)

    def project(block, rows):
        kv = jnp.dot(block, wkv[...], preferred_element_type=F32).astype(BF16)
        for i, row in enumerate(rows):
            piece = kv[i * TOK:(i + 1) * TOK]
            kall[row:row + TOK, :] = piece[:, :C]
            for p in range(PAIRS):
                vx[row:row + TOK, 256 * p:256 * p + 128] = piece[:, C + 128 * p:C + 128 * p + 128]

    def project_blocks(*blocks):
        rows = [sb[s, 0:TOK] if far == 0 else sb[s, TOK:2 * TOK] for far, s in blocks]
        project(rows[0] if len(rows) == 1 else jnp.concatenate(rows, axis=0), [ORDER.index(k) * TOK for k in blocks])

    loads[3].wait()
    loads[4].wait()
    project_blocks((0, 0))

    tot = st_send[0]
    for j, cp in enumerate(stat1):
        cp.wait_recv()
        tot = tot + st_recv[0, j]
    st_send[1] = tot
    stat2 = stat_copies(1)
    for cp in stat2:
        cp.start()
    y_first.wait_recv()
    send(2, 1)

    pe = iota((160, 256), 0)
    ps = iota((160, 256), 1)
    pi = lax.shift_right_logical(pe, 4)
    pj = pe & 15
    inner = (pi > 0) & (pi < 9)
    vert = ((pi > 0) | (r > 0)) & ((pi < 9) | (r < NZ - 1))
    left_src = jnp.where(pj > 0, pe - 1, jnp.where(inner, 167 + pi, jnp.where(pi == 0, 207, 239)))
    right_src = jnp.where(pj < 15, pe + 1, jnp.where(inner, 175 + pi, jnp.where(pi == 0, 208, 240)))
    left_ok = vert & ((pj > 0) | (c > 0))
    right_ok = vert & ((pj < 15) | (c < NCOL - 1))
    sel_left = jnp.where(left_ok & (ps == left_src), 1.0, 0.0).astype(BF16)
    sel_right = jnp.where(right_ok & (ps == right_src), 1.0, 0.0).astype(BF16)

    arrived(1, 1)
    send(1, 2)
    ys[1].start()
    ys[5].start()
    arrived(0, 1)
    send(0, 2)

    tot = st_send[1]
    for j, cp in enumerate(stat2):
        cp.wait_recv()
        tot = tot + st_recv[1, j]
    count = TOK * NZ * NCOL * per
    mom = tot * (1.0 / count)
    mean_g = mom[0:1]
    var_g = mom[1:2] - mean_g * mean_g
    rstd_g = lax.rsqrt(var_g + 1e-05)
    row8 = iota((8, 128), 0)
    both = jnp.where(row8 == 0, mean_g, jnp.where(row8 == 1, rstd_g, 0.0))
    hl = iota((128, C), 0) * per
    hc = iota((128, C), 1)
    gback = jnp.where((hc >= hl) & (hc < hl + per), 1.0, 0.0).astype(F32)
    wide = jnp.dot(both, gback, precision=HIGH, preferred_element_type=F32)
    xf = fresh[...].astype(F32)
    v = (xf - wide[0:1]) * wide[1:2] * ngain[...].reshape(1, C)
    ext[16:16 + TOK, :] = (v * (1.0 / (1.0 + jnp.exp(-v)))).astype(BF16)
    for cp in halos:
        cp.wait_recv()
    zero = jnp.zeros((16, C), BF16)
    ext[0:16, :] = jnp.where(r > 0, ext[0:16, :], zero)
    ext[144:160, :] = jnp.where(r < NZ - 1, ext[144:160, :], zero)
    whole = ext[...]
    e_left = jnp.dot(sel_left, whole, preferred_element_type=F32).astype(BF16)
    e_right = jnp.dot(sel_right, whole, preferred_element_type=F32).astype(BF16)
    for a in range(3):
        xw[:, (3 * a) * C:(3 * a + 1) * C] = e_left[16 * a:16 * a + TOK]
        xw[:, (3 * a + 1) * C:(3 * a + 2) * C] = ext[16 * a:16 * a + TOK, :]
        xw[:, (3 * a + 2) * C:(3 * a + 3) * C] = e_right[16 * a:16 * a + TOK]
    loads[5].wait()
    hidden = xf + jnp.dot(xw[...], wc[...], preferred_element_type=F32)
    hid[...] = hidden
    mean = jnp.mean(hidden, axis=-1, keepdims=True)
    cen = hidden - mean
    var = jnp.mean(cen * cen, axis=-1, keepdims=True)
    normed = (cen * lax.rsqrt(var + 1e-05) * again[...].reshape(1, C)).astype(BF16)
    loads[6].wait()
    q_mine[...] = (jnp.dot(normed, wq[...], preferred_element_type=F32) * (LOG2E / 8)).astype(BF16)
    q_cp = {j: remote(q_mine, q_recv.at[NX - j - 1], q_ssem.at[j - 1], q_rsem.at[NX - j - 1], {"col": xn[j]})
            for j in (1, 3, 2)}
    q_cp[3].start()
    q_cp[2].start()
    arrived(1, 2)
    send(1, 3)
    ys[2].start()
    ys[6].start()
    arrived(0, 2)
    send(0, 3)
    arrived(2, 1)
    send(2, 2)
    q_cp[1].start()
    project(normed, [0])

    lane = iota((TOK, 128), 1)

    def attend(slot, base, span, pairs=range(PAIRS), first=True, final=False, table=None):
        q_ref = q_mine if slot == 0 else q_recv.at[slot - 1]
        if table is None:
            table = jnp.zeros((TOK, 128), F32)
        for p in pairs:
            qp = q_ref[:, 128 * p:128 * p + 128]
            zq = jnp.zeros_like(qp)
            qm = jnp.concatenate([jnp.where(lane < HEAD, qp, zq), jnp.where(lane < HEAD, zq, qp)], axis=0)
            s = lax.dot_general(qm, kall[base:base + span, 128 * p:128 * p + 128], NT, preferred_element_type=F32)
            m = jnp.max(s, axis=1, keepdims=True)
            if not first:
                before = st_m[slot, p][:, :1]
                m = jnp.maximum(m, before)
            w = jnp.exp2(s - m).astype(BF16)
            o = jnp.dot(w, vx[base:base + span, 256 * p:256 * p + 256], preferred_element_type=F32)
            if not first:
                o = o + st_o[slot, p] * jnp.exp2(before - m)
            if not final:
                st_m[slot, p] = jnp.broadcast_to(m, (2 * TOK, 128))
                st_o[slot, p] = o
                continue
            den = o[:, 128:]
            norm = o[:, :128] / den
            part[slot, :, 128 * p:128 * p + 128] = jnp.where(lane < HEAD, norm[:TOK], norm[TOK:]).astype(BF16)
            ls = m + jnp.log2(den)
            table = jnp.where(lane == 2 * p, ls[:TOK], jnp.where(lane == 2 * p + 1, ls[TOK:], table))
        if final:
            lse[slot] = table.T[:16]
        return table

    project_blocks((0, 1), (0, 5), (0, 2), (0, 6))
    for s in (0, 1, 5):
        ys[s].wait_recv()
    project_blocks((1, 0), (1, 1), (1, 5))
    attend(0, 0, 8 * TOK)
    arrived(1, 3)
    send(1, 4)
    ys[3].start()
    ys[7].start()
    arrived(0, 3)
    send(0, 4)
    arrived(2, 2)
    send(2, 3)
    ys[2].wait_recv()
    ys[6].wait_recv()
    project_blocks((0, 3), (0, 7), (1, 2), (1, 6))
    q_cp[NX - 1].wait_recv()
    attend(1, TOK, 12 * TOK)
    arrived(1, 4)
    ys[4].start()
    arrived(0, 4)
    arrived(2, 3)
    send(2, 4)
    ys[3].wait_recv()
    ys[7].wait_recv()
    project_blocks((0, 4), (1, 3), (1, 7))
    q_cp[NX - 2].wait_recv()
    attend(2, TOK, 12 * TOK)
    arrived(2, 4)
    ys[4].wait_recv()
    project_blocks((1, 4))
    backs = []

    def give_back(j, g, at, wide_g):
        dst = NX - j - 1
        cp = remote(part.at[j, :, pl.ds(at, wide_g)], ret_a.at[dst, :, pl.ds(at, wide_g)],
                    a_ssem.at[j - 1, g], a_rsem.at[dst, g], {"col": xn[j]})
        cp.start()
        backs.append(cp)

    def give_lse(j):
        dst = NX - j - 1
        cp = remote(lse.at[j], ret_l.at[dst], l_ssem.at[j - 1], l_rsem.at[dst], {"col": xn[j]})
        cp.start()
        backs.append(cp)

    for j in (2, 1):
        attend(j, 13 * TOK, 4 * TOK, first=False, final=True)
        give_back(j, 0, 0, C)
        give_lse(j)
    q_cp[NX - 3].wait_recv()
    table = attend(3, TOK, 16 * TOK, range(0, 3), final=True)
    give_back(3, 0, 0, 384)
    attend(3, TOK, 16 * TOK, range(3, PAIRS), final=True, table=table)
    give_back(3, 1, 384, 256)
    give_lse(3)
    attend(0, 9 * TOK, 8 * TOK, first=False, final=True)
    for cp in backs:
        cp.wait_recv()

    ls = [lse[0]] + [ret_l[j] for j in range(3)]
    top_l = jnp.maximum(jnp.maximum(ls[0], ls[1]), jnp.maximum(ls[2], ls[3]))
    ws = [jnp.exp2(l - top_l) for l in ls]
    inv = 1.0 / (ws[0] + ws[1] + ws[2] + ws[3])
    eh = iota((32, C), 0) & 15
    ec = iota((32, C), 1)
    spread = jnp.where((ec >= eh * HEAD) & (ec < eh * HEAD + HEAD), 1.0, 0.0).astype(BF16)
    att = jnp.zeros((TOK, C), F32)
    for i in range(4):
        share = ws[i] * inv
        hi = share.astype(BF16)
        lo = (share - hi.astype(F32)).astype(BF16)
        split = jnp.concatenate([hi, lo], axis=0)
        full = lax.dot_general(split, spread, TN, preferred_element_type=F32)
        val = part[0] if i == 0 else ret_a[i - 1]
        att = att + full * val.astype(F32)
    loads[7].wait()
    out = hid[...] + jnp.dot(att.astype(BF16), wo[...], preferred_element_type=F32)
    out_ref[...] = out.astype(BF16)

    sends = stat1 + stat2 + halos + [y_first] + [cp for some in ring.values() for cp in some]
    sends += list(ys.values()) + list(q_cp.values()) + backs
    for cp in sends:
        cp.wait_send()


def on_device(fresh, stale_conv_in, stale_normed, norm_gain, conv_weight, attn_gain, w_query, w_key, w_value, w_out):
    shape = fresh.shape
    flat = lambda a: a.reshape(TOK, C)
    hbm = pl.BlockSpec(memory_space=pl.ANY)
    vmem = pl.BlockSpec(memory_space=pltpu.VMEM)
    dma = pltpu.SemaphoreType.DMA
    V = pltpu.VMEM
    out = pl.pallas_call(
        kernel,
        out_shape=jax.ShapeDtypeStruct((TOK, C), BF16),
        in_specs=[hbm] * 3 + [vmem] * 2 + [hbm] * 5,
        out_specs=vmem,
        scratch_shapes=[
            V((TOK, C), BF16), V((TOK, C), BF16), V((9 * C, C), BF16), V((C, C), BF16), V((C, 2 * C), BF16), V((C, C), BF16),
            V((2, 8, 128), F32), V((2, 7, 8, 128), F32),
            V((16, C), BF16), V((256, C), BF16), V((TOK, 9 * C), BF16),
            V((NZ, 2 * TOK, C), BF16), V((KROWS, C), BF16), V((KROWS, 256 * PAIRS), BF16), V((TOK, C), F32),
            V((TOK, C), BF16), V((3, TOK, C), BF16), V((4, TOK, C), BF16), V((3, TOK, C), BF16),
            V((4, 16, 128), F32), V((3, 16, 128), F32),
            V((4, PAIRS, 2 * TOK, 256), F32), V((4, PAIRS, 2 * TOK, 128), F32),
            dma((8,)), dma((2, 7)), dma((2, 7)), dma((8,)), dma((8,)),
            dma((3, 2, 4)), dma((3, 2, 4)), dma((9,)), dma((9,)),
            dma((3,)), dma((3,)), dma((3, 2)), dma((3, 2)), dma((3,)), dma((3,)),
        ],
        compiler_params=pltpu.CompilerParams(
            collective_id=0, has_side_effects=True, vmem_limit_bytes=60 * 2**20),
    )(
        flat(fresh), flat(stale_conv_in), flat(stale_normed),
        norm_gain, attn_gain,
        conv_weight.reshape(9 * C, C), w_query, w_key, w_value, w_out,
    )
    return out.reshape(shape)


def solution(mesh):
    cells = P(("img", "row"), "col", None)
    return jax.shard_map(
        on_device,
        mesh=mesh,
        in_specs=(cells, cells, cells) + (P(),) * 7,
        out_specs=cells,
        check_vma=False,
    )
```
